32 devices in a mesh: gx: 8 (over z, x), gy: 4 (over y, core).
Axes of the slice: x: 2, y: 2, z: 4, core: 2. Of those that a mesh axis runs over, the one named last changes fastest.
Arguments:
- inputs: float32 [64, 32, 16, 256], P('gx', 'gy'), may hold values from -6 to 6
- cotangent: float32 [64, 32, 16, 256], P('gx', 'gy'), may hold values from -6 to 6
- weight: float32 [6912, 256], replicated, may hold values from -0.125 to 0.125
- occupancy: int32 [64, 32, 16], P('gx', 'gy'), may hold values from 0 to 1, as said below
Outputs:
- input_grad: float32 [64, 32, 16, 256], P('gx', 'gy')
- weight_grad: float32 [6912, 256], P('gx', 'gy')
The draws below stay inside these ranges and needn't reach their ends.
Inputs may be any that keep to these rules, and one draw needn't show every extreme that they name: `occupancy`: occupied voxels lie in bricks of 8 x 8 x min(8, 16) voxels aligned to each device's block; some bricks are empty.
All inputs are finite; a program needn't handle non-finite values.
Results may differ from the reference program's by a relative error of at most 0.0001.
Values sent between devices are 32-bit elements; how exact they have to be, the bound alone decides.
No kernel may reach another device: no remote copies, remote signals or barrier semaphores. Data moves between devices by JAX's collectives and lax.ppermute only.
A program may use at most 192 MiB of HBM per device.

```python
import jax
import jax.numpy as jnp
from jax import lax

C = 256
CX = 8
CY = 8
NX = 64
NY = 32
NZ = 16


def draw_occupancy(key, part):
    brick_depth = min(8, NZ)
    count_x = NX // CX
    count_y = NY // CY
    count_z = NZ // brick_depth
    level_key = jax.random.fold_in(key, 11)
    brick_key = jax.random.fold_in(key, 12)
    dense_key = jax.random.fold_in(key, 13)
    voxel_key = jax.random.fold_in(key, 14)
    device_level = jax.random.randint(level_key, (count_x, count_y, 1), 3, 7)
    brick_score = jax.random.randint(brick_key, (count_x, count_y, count_z), 0, 10)
    brick_live = (brick_score < device_level).astype(jnp.int32)
    brick_dense = jax.random.randint(dense_key, (count_x, count_y, count_z), 1, 4) * brick_live
    dense_full = jnp.repeat(jnp.repeat(jnp.repeat(brick_dense, CX, axis=0), CY, axis=1), brick_depth, axis=2)
    voxel_score = jax.random.randint(voxel_key, (NX, NY, NZ), 0, 10)
    result = (voxel_score < dense_full).astype(jnp.int32)
    result = result.at[0, 0, 0].set(1)
    result = result.at[0, 0, 1].set(0)
    return result


def block_levels(own_key, shape, cuts, low, high):
    def one(position, shards_of):
        steps = jax.random.uniform(jax.random.fold_in(jax.random.fold_in(own_key, 6), position), (shards_of,), jnp.float32, low / len(cuts), high / len(cuts))
        return jnp.repeat(jnp.exp(steps), shape[position] // shards_of).reshape((-1,) + (1,) * (len(shape) - position - 1))

    level = one(*cuts[0])
    for cut in cuts[1:]:
        level = level * one(*cut)
    return level


def normal_values(rng, shape, deviation, most, pieces=(), dtype=jnp.bfloat16):
    gain = block_levels(rng, shape, pieces, -0.22, 0.18) if pieces else 1.0
    array = jax.random.normal(rng, shape, jnp.float32) * deviation * gain
    return jnp.minimum(jnp.maximum(array, -most), most).astype(dtype)


def setup_inputs(seed: int = 0) -> dict:
    key_of = jax.random.split(jax.random.key(seed), 5)
    return {
        "inputs": normal_values(key_of[0], (NX, NY, NZ, C), 1.0, 6.0, ((0, 8), (1, 4)), jnp.float32),
        "cotangent": normal_values(key_of[1], (NX, NY, NZ, C), 1.0, 6.0, ((0, 8), (1, 4)), jnp.float32),
        "weight": normal_values(key_of[2], (27 * C, C), (9 * C) ** -0.5, 0.125, (), jnp.float32),
        "occupancy": draw_occupancy(jax.random.fold_in(key_of[4], 71), 0),
    }


def offsets():
    return [(first, second, third) for first in range(3) for second in range(3) for third in range(3)]


def reference(inputs, cotangent, weight, occupancy):
    filled = occupancy.astype(jnp.float32)[..., None]
    masked = inputs * filled
    padded = jnp.pad(masked, ((1, 1), (1, 1), (1, 1), (0, 0)))
    total_rows = NX * NY * NZ
    preact = jnp.zeros((total_rows, C), jnp.float32)
    for index, (first, second, third) in enumerate(offsets()):
        piece = padded[first:first + NX, second:second + NY, third:third + NZ].reshape(total_rows, C)
        preact = preact + jnp.dot(piece, weight[index * C:(index + 1) * C], precision=lax.Precision.HIGHEST, preferred_element_type=jnp.float32)
    sigma = jax.nn.sigmoid(preact)
    upstream = cotangent.reshape(total_rows, C) * sigma * (1.0 + preact * (1.0 - sigma)) * filled.reshape(total_rows, 1)
    grid_up = jnp.pad(upstream.reshape(NX, NY, NZ, C), ((1, 1), (1, 1), (1, 1), (0, 0)))
    result = jnp.zeros((total_rows, C), jnp.float32)
    blocks = []
    for index, (first, second, third) in enumerate(offsets()):
        kernel = weight[index * C:(index + 1) * C]
        back = grid_up[2 - first:2 - first + NX, 2 - second:2 - second + NY, 2 - third:2 - third + NZ].reshape(total_rows, C)
        result = result + jnp.dot(back, kernel.T, precision=lax.Precision.HIGHEST, preferred_element_type=jnp.float32)
        piece = padded[first:first + NX, second:second + NY, third:third + NZ].reshape(total_rows, C)
        blocks.append(jnp.dot(piece.T, upstream, precision=lax.Precision.HIGHEST, preferred_element_type=jnp.float32))
    input_grad = (result * filled.reshape(total_rows, 1)).reshape(NX, NY, NZ, C)
    return input_grad, jnp.concatenate(blocks, axis=0)
```

```python
import jax
import jax.numpy as jnp
from jax import lax
from jax.experimental import pallas as pl
from jax.experimental.pallas import tpu as pltpu
from jax.sharding import PartitionSpec as P

F32 = jnp.float32
BF16 = jnp.bfloat16
VMEM_BYTES = 40 * 1024 * 1024
LANES = 128


def split(value):
    high = value.astype(BF16)
    low = (value - high.astype(F32)).astype(BF16)
    return high, low


def with_halo(array, sides, width):
    for axis, dim in sides:
        devices, length = (lax.axis_size(axis), array.shape[dim])
        up = [(i, (i + 1) % devices) for i in range(devices - 1)]
        down = [(j, i) for i, j in up]
        last = lax.slice_in_dim(array, length - width, length, axis=dim)
        first = lax.slice_in_dim(array, 0, width, axis=dim)
        before = lax.ppermute(last, axis, up)
        after = lax.ppermute(first, axis, down)
        array = jnp.concatenate([before, array, after], axis=dim)
    return array


def shift_rows(value, step, depth):
    rows = value.shape[0]
    place = lax.broadcasted_iota(jnp.int32, value.shape, 0) % depth
    moved = pltpu.roll(value, (-step) % rows, 0)
    inside = (place + step >= 0) & (place + step < depth)
    return jnp.where(inside, moved, 0.0)


def stack_terms(value):
    high, low = split(value)
    return jnp.concatenate([high, low, high], axis=-1)


def forward_kernel(span_x, span_y, depth, padded_ref, cot_ref, weight_ref, up_ref, stack_ref, acc_ref):
    step = pl.program_id(0)
    count = span_x * span_y * depth
    channels = weight_ref.shape[-1]

    @pl.when(step == 0)
    def _():
        for i in range(span_x + 2):
            stack_ref[i] = stack_terms(padded_ref[i])
        acc_ref[...] = jnp.zeros_like(acc_ref)

    first, second = step // 3, step % 3
    piece = stack_ref[pl.ds(first, span_x), pl.ds(second, span_y)].reshape(count, 3 * channels)
    for third in range(3):
        high, low = split(weight_ref[third])
        acc_ref[third] += jnp.dot(
            piece, jnp.concatenate([high, high, low], axis=0), preferred_element_type=F32
        )

    @pl.when(step == 8)
    def _():
        preact = (
            acc_ref[1] + shift_rows(acc_ref[0], -1, depth) + shift_rows(acc_ref[2], 1, depth)
        )
        sigma = jax.nn.sigmoid(preact)
        up_ref[...] = cot_ref[...] * sigma * (1.0 + preact * (1.0 - sigma))


def forward(padded, cot, weight, span_x, span_y, depth):
    channels = padded.shape[-1]
    count = span_x * span_y * depth

    def kernel(*refs):
        forward_kernel(span_x, span_y, depth, *refs)

    return pl.pallas_call(
        kernel,
        grid=(9,),
        in_specs=[
            pl.BlockSpec(padded.shape, lambda s: (0, 0, 0, 0)),
            pl.BlockSpec((count, channels), lambda s: (0, 0)),
            pl.BlockSpec((3, channels, channels), lambda s: (s, 0, 0)),
        ],
        out_specs=pl.BlockSpec((count, channels), lambda s: (0, 0)),
        out_shape=jax.ShapeDtypeStruct((count, channels), F32),
        scratch_shapes=[
            pltpu.VMEM((span_x + 2, span_y + 2, depth, 3 * channels), BF16),
            pltpu.VMEM((3, count, channels), F32),
        ],
        compiler_params=pltpu.CompilerParams(vmem_limit_bytes=VMEM_BYTES),
        cost_estimate=pl.CostEstimate(
            flops=2 * 81 * count * channels * channels,
            bytes_accessed=4 * (padded.size + 2 * cot.size + weight.size),
            transcendentals=count * channels,
        ),
    )(padded, cot, weight)


def data_kernel(span_x, span_y, depth, padded_ref, filled_ref, weight_ref, out_ref, stack_ref, acc_ref):
    step = pl.program_id(0)
    count = span_x * span_y * depth
    channels = weight_ref.shape[-1]

    @pl.when(step == 0)
    def _():
        for i in range(span_x + 2):
            stack_ref[i] = stack_terms(padded_ref[i])
        acc_ref[...] = jnp.zeros_like(acc_ref)

    first, second = step // 3, step % 3
    piece = stack_ref[pl.ds(2 - first, span_x), pl.ds(2 - second, span_y)].reshape(
        count, 3 * channels
    )
    for third in range(3):
        high, low = split(weight_ref[third])
        acc_ref[third] += lax.dot_general(
            piece,
            jnp.concatenate([high, high, low], axis=1),
            (((1,), (1,)), ((), ())),
            preferred_element_type=F32,
        )

    @pl.when(step == 8)
    def _():
        total = acc_ref[1] + shift_rows(acc_ref[0], 1, depth) + shift_rows(acc_ref[2], -1, depth)
        out_ref[...] = total * filled_ref[...]


def data_grad(padded, filled, weight, span_x, span_y, depth):
    channels = padded.shape[-1]
    count = span_x * span_y * depth

    def kernel(*refs):
        data_kernel(span_x, span_y, depth, *refs)

    return pl.pallas_call(
        kernel,
        grid=(9,),
        in_specs=[
            pl.BlockSpec(padded.shape, lambda s: (0, 0, 0, 0)),
            pl.BlockSpec((count, 1), lambda s: (0, 0)),
            pl.BlockSpec((3, channels, channels), lambda s: (s, 0, 0)),
        ],
        out_specs=pl.BlockSpec((count, channels), lambda s: (0, 0)),
        out_shape=jax.ShapeDtypeStruct((count, channels), F32),
        scratch_shapes=[
            pltpu.VMEM((span_x + 2, span_y + 2, depth, 3 * channels), BF16),
            pltpu.VMEM((3, count, channels), F32),
        ],
        compiler_params=pltpu.CompilerParams(vmem_limit_bytes=VMEM_BYTES),
        cost_estimate=pl.CostEstimate(
            flops=2 * 81 * count * channels * channels,
            bytes_accessed=4 * (padded.size + count * channels + weight.size),
            transcendentals=0,
        ),
    )(padded, filled, weight)


def filter_kernel(span_x, span_y, depth, parts, place_ref, padded_ref, up_ref, *refs):
    outs, (turned_ref, left_ref, right_ref, acc_ref) = refs[: 2 * parts], refs[2 * parts :]
    channels = padded_ref.shape[-1]
    count = span_x * span_y * depth
    slab = span_y * depth
    groups = channels // (16 * parts)
    rows = groups * 16

    left, right = up_ref[:, :LANES], up_ref[:, LANES:]
    swap_high, swap_low = place_ref[0, 0] > 0, place_ref[0, 1] > 0
    left, right = jnp.where(swap_high, right, left), jnp.where(swap_high, left, right)
    left = jnp.where(swap_low, pltpu.roll(left, 64, 1), left)
    right = jnp.where(swap_low, pltpu.roll(right, 64, 1), right)
    upstream = jnp.concatenate([left, right], axis=1)
    for third in range(3):
        high, low = split(shift_rows(upstream, 1 - third, depth))
        right_ref[third, :count] = high
        right_ref[third, count : 2 * count] = high
        right_ref[third, 2 * count :] = low

    for second in range(3):
        for i in range(span_x + 2):
            piece = padded_ref[i, second : second + span_y].reshape(slab, channels)
            high, low = split(piece.T)
            turned_ref[0, second, :, i * slab : (i + 1) * slab] = high
            turned_ref[1, second, :, i * slab : (i + 1) * slab] = low

    low_lanes = lax.broadcasted_iota(jnp.int32, (8, LANES), 1) < 64
    for part in range(parts):
        for first in range(3):
            for second in range(3):
                tap = first * 3 + second
                lanes = slice(first * slab, first * slab + count)
                for group in range(groups):
                    source = slice((group * parts + part) * 16, (group * parts + part + 1) * 16)
                    target = slice(tap * rows + group * 16, tap * rows + (group + 1) * 16)
                    high = turned_ref[0, second, source, lanes]
                    left_ref[target, :count] = high
                    left_ref[target, count : 2 * count] = turned_ref[1, second, source, lanes]
                    left_ref[target, 2 * count :] = high
        keep_ref, send_ref = outs[2 * part], outs[2 * part + 1]
        jump = place_ref[0, 2 + part]

        def one(third, carry):
            acc_ref[...] = jnp.dot(left_ref[...], right_ref[third], preferred_element_type=F32)
            for tap in range(9):
                for group in range(groups):
                    at = place_ref[1 + part, (tap * 3 + third) * groups + group]
                    start = tap * rows + group * 16
                    for high_half in range(2):
                        columns = slice(high_half * LANES, (high_half + 1) * LANES)
                        upper = acc_ref[start : start + 8, columns]
                        lower = acc_ref[start + 8 : start + 16, columns]
                        keep_ref[at + high_half * jump] = jnp.where(
                            low_lanes, upper, pltpu.roll(lower, 64, 1)
                        )
                        send_ref[at + high_half * jump] = jnp.where(
                            low_lanes, pltpu.roll(upper, 64, 1), lower
                        )
            return carry

        lax.fori_loop(0, 3, one, 0)


def filter_terms(padded, upstream, place, parts, chunks, units, span_x, span_y, depth):
    channels = padded.shape[-1]
    count = span_x * span_y * depth

    def kernel(*refs):
        filter_kernel(span_x, span_y, depth, parts, *refs)

    whole = pl.BlockSpec(memory_space=pltpu.VMEM)
    shape = jax.ShapeDtypeStruct((chunks * units, 8, LANES), F32)
    return pl.pallas_call(
        kernel,
        in_specs=[pl.BlockSpec(memory_space=pltpu.SMEM), whole, whole],
        out_specs=[whole] * (2 * parts),
        out_shape=[shape] * (2 * parts),
        scratch_shapes=[
            pltpu.VMEM((2, 3, channels, (span_x + 2) * span_y * depth), BF16),
            pltpu.VMEM((9 * channels // parts, 3 * count), BF16),
            pltpu.VMEM((3, 3 * count, channels), BF16),
            pltpu.VMEM((9 * channels // parts, channels), F32),
        ],
        compiler_params=pltpu.CompilerParams(vmem_limit_bytes=VMEM_BYTES),
        cost_estimate=pl.CostEstimate(
            flops=2 * 81 * count * channels * channels,
            bytes_accessed=4 * (padded.size + upstream.size + 27 * channels * channels),
            transcendentals=0,
        ),
    )(place, padded, upstream)


def bits_of(size):
    return size.bit_length() - 1


def reduce_part(keep, send, stages, units):
    axis, bit = stages[0]
    for index, (axis, bit) in enumerate(stages):
        pairs = [(i, i ^ (1 << bit)) for i in range(lax.axis_size(axis))]
        got = lax.ppermute(send, axis, pairs)
        if index == len(stages) - 1:
            return keep + got
        middle = keep.shape[0] // 2
        send = keep[middle:] + got[middle:]
        keep = keep[:middle] + got[:middle]


def plain_filter_grad(bordered, upstream, span_x, span_y, depth):
    padded = jnp.pad(bordered, ((0, 0), (0, 0), (1, 1), (0, 0)))
    blocks = []
    for first in range(3):
        for second in range(3):
            for third in range(3):
                piece = padded[
                    first : first + span_x, second : second + span_y, third : third + depth
                ].reshape(upstream.shape)
                blocks.append(
                    jnp.dot(
                        piece.T,
                        upstream,
                        precision=lax.Precision.HIGHEST,
                        preferred_element_type=F32,
                    )
                )
    term = jnp.concatenate(blocks, axis=0)
    row_sums = lax.psum_scatter(term, "gx", scatter_dimension=0, tiled=True)
    return lax.psum_scatter(row_sums, "gy", scatter_dimension=1, tiled=True)


def data_part(upstream, shape, filled, taps, sides):
    span_x, span_y, depth, channels = shape
    border_up = with_halo(upstream.reshape(shape), sides, 1)
    result = data_grad(border_up, filled.reshape(-1, 1), taps, span_x, span_y, depth)
    return result.reshape(shape)


def body(inputs, cotangent, weight, occupancy):
    span_x, span_y, depth, channels = inputs.shape
    count = span_x * span_y * depth
    size_x, size_y = lax.axis_size("gx"), lax.axis_size("gy")
    sides = (("gx", 0), ("gy", 1))
    filled = occupancy.astype(F32)[..., None]
    masked = inputs * filled
    bordered = with_halo(masked, sides, 1)
    cot = (cotangent * filled).reshape(count, channels)
    taps = weight.reshape(27, channels, channels)
    upstream = forward(bordered, cot, taps, span_x, span_y, depth)

    parts, groups = 2, channels // 32
    if channels // size_y != 64 or 27 * groups % size_x or channels != 256:
        weight_grad = plain_filter_grad(bordered, upstream, span_x, span_y, depth)
        return (data_part(upstream, inputs.shape, filled, taps, sides), weight_grad)
    units = 27 * groups // size_x
    me_x, me_y = lax.axis_index("gx"), lax.axis_index("gy")
    bits_x, bits_y = bits_of(size_x), bits_of(size_y)
    order = {
        0: [("gy", 0), ("gx", 0), ("gy", 1)] + [("gx", b) for b in range(1, bits_x)],
        1: [("gy", 0), ("gy", 1)] + [("gx", b) for b in range(bits_x)],
    }
    unit = jnp.arange(27 * groups, dtype=jnp.int32)
    relative = (unit // units) ^ me_x
    rows = []
    jumps = []
    for part in range(parts):
        stages = order[part][1:]
        at = jnp.zeros_like(unit)
        for position, (axis, bit) in enumerate(stages):
            worth = 1 << (len(stages) - 1 - position)
            if axis == "gx":
                at = at + ((relative >> bit) & 1) * worth
            else:
                jumps.append(jnp.int32(worth * units))
        rows.append(at * units + unit % units)
    head = jnp.stack([(me_y >> 1) & 1, me_y & 1] + jumps).astype(jnp.int32)
    head = jnp.pad(head, (0, unit.size - head.size))
    place = jnp.stack([head] + rows)
    chunks = 2 * size_x
    terms = filter_terms(
        bordered, upstream, place, parts, chunks, units, span_x, span_y, depth
    )
    sums = [
        reduce_part(terms[2 * p], terms[2 * p + 1], order[p], units) for p in range(parts)
    ]
    both = jnp.stack([s.reshape(units, 8, 2, 64) for s in sums], axis=1)
    weight_grad = both.transpose(0, 1, 3, 2, 4).reshape(units * 32, 64)

    return (data_part(upstream, inputs.shape, filled, taps, sides), weight_grad)


def solution(mesh):
    in_specs = (P("gx", "gy", None, None), P("gx", "gy", None, None), P(), P("gx", "gy", None))
    out_specs = (P("gx", "gy", None, None), P("gx", "gy"))
    return jax.shard_map(body, mesh=mesh, in_specs=in_specs, out_specs=out_specs, check_vma=False)
```

```python
import jax
import jax.numpy as jnp
import numpy as np
from jax import lax
from jax.experimental import pallas as pl
from jax.experimental.pallas import tpu as pltpu
from jax.sharding import PartitionSpec as P

F32 = jnp.float32
BF16 = jnp.bfloat16
LANES = 128


def split(value):
    high = value.astype(BF16)
    low = (value - high.astype(F32)).astype(BF16)
    return high, low


def shift_rows(value, step, depth):
    rows = value.shape[0]
    place = lax.broadcasted_iota(jnp.int32, value.shape, 0) % depth
    moved = pltpu.roll(value, (-step) % rows, 0)
    inside = (place + step >= 0) & (place + step < depth)
    return jnp.where(inside, moved, 0.0)


def stack_terms(value):
    return jnp.concatenate(split(value), axis=-1)


def products(piece, high, low, dim):
    channels = high.shape[0]

    def dot(left, right):
        return lax.dot_general(
            left, right, (((1,), (dim,)), ((), ())), preferred_element_type=F32
        )

    own_high, own_low = piece[:, :channels], piece[:, channels:]
    return dot(own_high, high) + dot(own_low, high) + dot(own_high, low)


WHOLE = pl.BlockSpec(memory_space=pltpu.VMEM)


def params(mib):
    return pltpu.CompilerParams(vmem_limit_bytes=mib * 1024 * 1024)


def padded_slab(index, span, own, before_x, after_x, before_y, after_y):
    if index == 0:
        middle = before_x[0]
    elif index == span + 1:
        middle = after_x[0]
    else:
        middle = own(index - 1)
    return jnp.concatenate([before_y[index], middle, after_y[index]], axis=0)


def forward_kernel(
    swap_ref,
    inputs_ref,
    filled_ref,
    before_x_ref,
    after_x_ref,
    before_y_ref,
    after_y_ref,
    cot_ref,
    weight_ref,
    up_ref,
    turned_ref,
    right_ref,
    stack_ref,
    acc_ref,
    slab_ref,
):
    step = pl.program_id(0)
    span_x, span_y, depth, channels = inputs_ref.shape
    count, side = span_x * span_y * depth, span_y * depth

    @pl.when(step == 0)
    def _():
        for i in range(span_x + 2):
            slab = padded_slab(
                i,
                span_x,
                lambda x: inputs_ref[x] * filled_ref[x],
                before_x_ref,
                after_x_ref,
                before_y_ref,
                after_y_ref,
            )
            slab_ref[i] = slab
            stack_ref[i] = stack_terms(slab)
        acc_ref[...] = jnp.zeros_like(acc_ref)

    first, second = step // 3, step % 3
    piece = stack_ref[pl.ds(first, span_x), pl.ds(second, span_y)].reshape(count, 2 * channels)
    for third in range(3):
        acc_ref[third] += products(piece, *split(weight_ref[3 * step + third]), 0)

    each = -(-(span_x + 2) // 3)
    groups = channels // 16
    for j in range(each):
        i = jnp.minimum(first * each + j, span_x + 1)
        turn = slab_ref[i, pl.ds(second, span_y)].reshape(side, channels).T
        high, low = split(turn)
        lanes = pl.ds(pl.multiple_of(i * side, LANES), side)
        for m in range(groups):
            at = (m % 2) * 3 * (channels // 2) + 16 * (m // 2)
            rows = pl.ds(pl.multiple_of(at + second * (channels // 2), 16), 16)
            turned_ref[0, rows, lanes] = high[16 * m : 16 * m + 16]
            turned_ref[1, rows, lanes] = low[16 * m : 16 * m + 16]

    @pl.when(step == 8)
    def _():
        preact = (
            acc_ref[1] + shift_rows(acc_ref[0], -1, depth) + shift_rows(acc_ref[2], 1, depth)
        )
        sigma = jax.nn.sigmoid(preact)
        cot = cot_ref[...] * filled_ref[...].reshape(count, 1)
        upstream = cot * sigma * (1.0 + preact * (1.0 - sigma))
        up_ref[...] = upstream

        left, right = upstream[:, :LANES], upstream[:, LANES:]
        swap_high, swap_low = swap_ref[0] > 0, swap_ref[1] > 0
        left, right = jnp.where(swap_high, right, left), jnp.where(swap_high, left, right)
        left = jnp.where(swap_low, pltpu.roll(left, 64, 1), left)
        right = jnp.where(swap_low, pltpu.roll(right, 64, 1), right)
        ordered = jnp.concatenate([left, right], axis=1)
        for third in range(3):
            high, low = split(shift_rows(ordered, 1 - third, depth))
            right_ref[third, 0] = high
            right_ref[third, 1] = low


def forward(swap, inputs, filled, before_x, after_x, before_y, after_y, cot, taps):
    span_x, span_y, depth, channels = inputs.shape
    count = span_x * span_y * depth
    turned = (2, 3 * channels, (span_x + 2) * span_y * depth)
    right = (3, 2, count, channels)
    return pl.pallas_call(
        forward_kernel,
        grid=(9,),
        in_specs=[pl.BlockSpec(memory_space=pltpu.SMEM)]
        + [WHOLE] * 8,
        out_specs=[WHOLE] * 3,
        out_shape=[
            jax.ShapeDtypeStruct((count, channels), F32),
            jax.ShapeDtypeStruct(turned, BF16),
            jax.ShapeDtypeStruct(right, BF16),
        ],
        scratch_shapes=[
            pltpu.VMEM((span_x + 2, span_y + 2, depth, 2 * channels), BF16),
            pltpu.VMEM((3, count, channels), F32),
            pltpu.VMEM((span_x + 2, span_y + 2, depth, channels), F32),
        ],
        compiler_params=params(24),
        cost_estimate=pl.CostEstimate(
            flops=2 * 81 * count * channels * channels,
            bytes_accessed=4 * (8 * inputs.size + taps.size),
            transcendentals=count * channels,
        ),
    )(swap, inputs, filled, before_x, after_x, before_y, after_y, cot, taps)


def filter_kernel(part, side, place_ref, turned_ref, right_ref, keep_ref, send_ref, acc_ref):
    count, channels = right_ref.shape[2:]
    low_lanes = lax.broadcasted_iota(jnp.int32, (8, LANES), 1) < 64
    keep_jump, send_jump = place_ref[0, 0], place_ref[1, 0]
    seen = 0
    rows = 3 * (channels // 2)
    base = part * rows
    for third in range(3):
        for first in range(3):
            lanes = slice(first * side, first * side + count)
            high = turned_ref[0, base : base + rows, lanes]
            low = turned_ref[1, base : base + rows, lanes]
            acc_ref[...] = (
                jnp.dot(high, right_ref[third, 0], preferred_element_type=F32)
                + jnp.dot(low, right_ref[third, 0], preferred_element_type=F32)
                + jnp.dot(high, right_ref[third, 1], preferred_element_type=F32)
            )
            for group in range(rows // 16):
                keep_at, send_at = place_ref[0, 1 + seen], place_ref[1, 1 + seen]
                seen += 1
                start = group * 16
                for high_half in range(2):
                    columns = slice(high_half * LANES, (high_half + 1) * LANES)
                    upper = acc_ref[start : start + 8, columns]
                    lower = acc_ref[start + 8 : start + 16, columns]
                    keep_ref[keep_at + high_half * keep_jump] = jnp.where(
                        low_lanes, upper, pltpu.roll(lower, 64, 1)
                    )
                    send_ref[send_at + high_half * send_jump] = jnp.where(
                        low_lanes, pltpu.roll(upper, 64, 1), lower
                    )


def filter_terms(part, place, turned, right, tiles, side):
    count, channels = right.shape[2:]

    def kernel(*refs):
        filter_kernel(part, side, *refs)

    shape = jax.ShapeDtypeStruct((tiles, 8, LANES), F32)
    return pl.pallas_call(
        kernel,
        in_specs=[pl.BlockSpec(memory_space=pltpu.SMEM), WHOLE, WHOLE],
        out_specs=[WHOLE] * 2,
        out_shape=[shape] * 2,
        scratch_shapes=[pltpu.VMEM((3 * channels // 2, channels), F32)],
        compiler_params=params(12),
        cost_estimate=pl.CostEstimate(
            flops=81 * count * channels * channels,
            bytes_accessed=2 * (turned.size + right.size) + 8 * tiles * 8 * LANES,
            transcendentals=0,
        ),
    )(place, turned, right)


def unit_tables(channels, size_x):
    groups = channels // 16
    units = 27 * groups // size_x
    tables = []
    for part in range(2):
        order = [
            (first * 9 + second * 3 + third) * groups + m
            for third in range(3)
            for first in range(3)
            for second in range(3)
            for m in range(part, groups, 2)
        ]
        unit = np.array(order, np.int32)
        tables.append((unit // units, unit % units // 2))
    return tables


def data_kernel(
    begin,
    end,
    turn_ref,
    up_ref,
    filled_ref,
    before_x_ref,
    after_x_ref,
    before_y_ref,
    after_y_ref,
    weight_ref,
    out_ref,
    stack_ref,
    acc_ref,
):
    step = pl.program_id(0)
    span_x, span_y, depth, channels = up_ref.shape
    width = end - begin
    count = width * span_y * depth

    @pl.when(step == 0)
    def _():
        for i in range(width + 2):
            stack_ref[i] = stack_terms(
                padded_slab(
                    begin + i,
                    span_x,
                    lambda x: up_ref[x],
                    before_x_ref,
                    after_x_ref,
                    before_y_ref,
                    after_y_ref,
                )
            )
        acc_ref[...] = jnp.zeros_like(acc_ref)

    first, second = step // 3, step % 3
    piece = stack_ref[pl.ds(2 - first, width), pl.ds(2 - second, span_y)].reshape(
        count, 2 * channels
    )
    for third in range(3):
        acc_ref[third] += products(piece, *split(weight_ref[3 * step + third]), 1)

    @pl.when(step == 8)
    def _():
        total = acc_ref[1] + shift_rows(acc_ref[0], 1, depth) + shift_rows(acc_ref[2], -1, depth)
        out_ref[...] = total * filled_ref[begin:end].reshape(count, 1)


def data_grad(turn, up, filled, before_x, after_x, before_y, after_y, taps, begin, end):
    span_x, span_y, depth, channels = up.shape
    width = end - begin
    count = width * span_y * depth

    def kernel(*refs):
        data_kernel(begin, end, *refs)

    return pl.pallas_call(
        kernel,
        grid=(9,),
        in_specs=[pl.BlockSpec(memory_space=pltpu.SMEM)] + [WHOLE] * 7,
        out_specs=WHOLE,
        out_shape=jax.ShapeDtypeStruct((count, channels), F32),
        scratch_shapes=[
            pltpu.VMEM((width + 2, span_y + 2, depth, 2 * channels), BF16),
            pltpu.VMEM((3, count, channels), F32),
        ],
        compiler_params=params(16),
        cost_estimate=pl.CostEstimate(
            flops=2 * 81 * count * channels * channels,
            bytes_accessed=4 * (3 * count * channels + taps.size),
            transcendentals=0,
        ),
    )(turn, up, filled, before_x, after_x, before_y, after_y, taps)


def bits_of(size):
    return size.bit_length() - 1


def after(value, *others):
    return lax.optimization_barrier((value, *others))[0]


def neighbours(axis):
    size = lax.axis_size(axis)
    up = [(i, i + 1) for i in range(size - 1)]
    return up, [(j, i) for i, j in up]


def halo_x(first, last):
    up, down = neighbours("gx")
    return lax.ppermute(last, "gx", up), lax.ppermute(first, "gx", down)


def halo_y(first, last, before_x, after_x):
    up, down = neighbours("gy")
    span_y = before_x.shape[1]
    low = jnp.concatenate([before_x[:, 0], first, after_x[:, 0]], axis=0)
    high = jnp.concatenate([before_x[:, span_y - 1], last, after_x[:, span_y - 1]], axis=0)
    got = lax.ppermute(high[:, None], "gy", up), lax.ppermute(low[:, None], "gy", down)
    return got


def flip_pairs(size_x, size_y, flips):
    pairs = []
    for x in range(size_x):
        for y in range(size_y):
            axis, bit = flips[y & 1]
            other = (x ^ (1 << bit), y) if axis == "gx" else (x, y ^ (1 << bit))
            pairs.append((x * size_y + y, other[0] * size_y + other[1]))
    return pairs


def plain_filter_grad(bordered, upstream, span_x, span_y, depth):
    padded = jnp.pad(bordered, ((0, 0), (0, 0), (1, 1), (0, 0)))
    blocks = []
    for first in range(3):
        for second in range(3):
            for third in range(3):
                piece = padded[
                    first : first + span_x, second : second + span_y, third : third + depth
                ].reshape(upstream.shape)
                blocks.append(
                    jnp.dot(
                        piece.T,
                        upstream,
                        precision=lax.Precision.HIGHEST,
                        preferred_element_type=F32,
                    )
                )
    term = jnp.concatenate(blocks, axis=0)
    row_sums = lax.psum_scatter(term, "gx", scatter_dimension=0, tiled=True)
    return lax.psum_scatter(row_sums, "gy", scatter_dimension=1, tiled=True)


def body(inputs, cotangent, weight, occupancy):
    span_x, span_y, depth, channels = inputs.shape
    count = span_x * span_y * depth
    size_x, size_y = lax.axis_size("gx"), lax.axis_size("gy")
    me_x, me_y = lax.axis_index("gx"), lax.axis_index("gy")
    filled = occupancy.astype(F32)[..., None]
    taps = weight.reshape(27, channels, channels)
    cot = cotangent.reshape(count, channels)

    def masked(x, y):
        return inputs[x, y] * filled[x, y]

    every = slice(None)
    last_x, last_y = span_x - 1, span_y - 1
    face, other_face = masked(slice(0, 1), every), masked(slice(last_x, span_x), every)
    before_x, after_x = halo_x(face, other_face)
    before_y, after_y = halo_y(masked(every, 0), masked(every, last_y), before_x, after_x)
    swap = jnp.stack([(me_y >> 1) & 1, me_y & 1]).astype(jnp.int32)
    upstream, turned, right = forward(
        swap,
        inputs,
        filled,
        before_x,
        after_x,
        before_y.reshape(span_x + 2, 1, depth, channels),
        after_y.reshape(span_x + 2, 1, depth, channels),
        cot,
        taps,
    )
    up = upstream.reshape(inputs.shape)

    def data_halo_x(*others):
        first, last = up[:1], up[last_x:]
        for other in others:
            first, last, _ = lax.optimization_barrier((first, last, other))
        return halo_x(first, last)

    def data_halo_y(sides, *others):
        first, last = up[:, 0], up[:, last_y]
        for other in others:
            first, last, _ = lax.optimization_barrier((first, last, other))
        return halo_y(first, last, *sides)

    def data_piece(turn, sides, ends, begin, end):
        return data_grad(turn, up, filled, *sides, *ends, taps, begin, end)

    middle = span_x // 2
    parts, groups = 2, channels // 16
    if channels // size_y != 64 or 27 * groups % (parts * size_x) or channels != 256:
        own = inputs * filled
        bordered = jnp.concatenate(
            [before_y, jnp.concatenate([before_x, own, after_x], axis=0), after_y], axis=1
        )
        weight_grad = plain_filter_grad(bordered, upstream, span_x, span_y, depth)
        sides = data_halo_x()
        result = data_piece(swap, sides, data_halo_y(sides), 0, span_x)
        return (result.reshape(inputs.shape), weight_grad)

    units = 27 * groups // size_x // parts
    rest = [("gx", b) for b in range(1, bits_of(size_x))]
    x_bit, y_bit = ("gx", 0), ("gy", 1)
    paths = [
        ([x_bit, y_bit] + rest, [y_bit, x_bit] + rest),
        ([y_bit, x_bit] + rest, rest + [x_bit, y_bit]),
    ]
    tiles = 2 * size_x * units
    core = [(i, i ^ 1) for i in range(size_y)]
    tables = []
    for part, (chunk, place) in enumerate(unit_tables(channels, size_x)):
        relative = jnp.asarray(chunk) ^ me_x
        ways = []
        for path in paths[part]:
            at, jump = jnp.zeros_like(relative), 0
            for position, (axis, bit) in enumerate(path):
                worth = 1 << (len(path) - 1 - position)
                if axis == "gx":
                    at = at + ((relative >> bit) & 1) * worth
                else:
                    jump = worth * units
            at = at * units + jnp.asarray(place)
            ways.append(jnp.concatenate([jnp.full((1,), jump, jnp.int32), at]))
        tables.append(jnp.where(me_y & 1, jnp.stack(ways[::-1]), jnp.stack(ways)))
    flips = [list(zip(*path)) for path in paths]
    stages = len(flips[0])

    def terms(part, table):
        keep, send = filter_terms(part, table, turned, right, tiles, span_y * depth)
        return keep, send, lax.ppermute(send, "gy", core)

    def stage(part, index, keep, got):
        half = keep.shape[0] // 2
        send, keep = keep[half:] + got[half:], keep[:half] + got[:half]
        pairs = flip_pairs(size_x, size_y, flips[part][index])
        return keep, send, lax.ppermute(send, ("gx", "gy"), pairs)

    keep_a, send_a, got_a = terms(0, tables[0])
    sides = data_halo_x(send_a)
    keep_a, send_a, got_a = stage(0, 0, keep_a, got_a)
    keep_b, send_b, got_b = terms(1, after(tables[1], send_a, *sides))
    ends = data_halo_y(sides, send_b)
    keep_b, send_b, got_b = stage(1, 0, keep_b, got_b)
    keep_a, send_a, got_a = stage(0, 1, keep_a, got_a)
    pieces = []
    for index in range(2, stages):
        if index < 4:
            begin, end = ((0, middle), (middle, span_x))[index - 2]
            pieces.append(data_piece(after(swap, send_a, send_b), sides, ends, begin, end))
            keep_a, keep_b = after(keep_a, pieces[-1]), after(keep_b, pieces[-1])
        keep_a, send_a, got_a = stage(0, index, keep_a, got_a)
        keep_b, send_b, got_b = stage(1, index - 1, keep_b, got_b)
    keep_b, send_b, got_b = stage(1, stages - 1, keep_b, got_b)
    sums = [keep_a + got_a, keep_b + got_b]
    both = jnp.stack([s.reshape(units, 8, 2, 64) for s in sums], axis=1)
    weight_grad = both.transpose(0, 1, 3, 2, 4).reshape(units * 32, 64)
    return (jnp.concatenate(pieces, axis=0).reshape(inputs.shape), weight_grad)


def solution(mesh):
    in_specs = (P("gx", "gy", None, None), P("gx", "gy", None, None), P(), P("gx", "gy", None))
    out_specs = (P("gx", "gy", None, None), P("gx", "gy"))
    return jax.shard_map(body, mesh=mesh, in_specs=in_specs, out_specs=out_specs, check_vma=False)
```

```python
import jax
import jax.numpy as jnp
import numpy as np
from jax import lax
from jax.experimental import pallas as pl
from jax.experimental.pallas import tpu as pltpu
from jax.sharding import PartitionSpec as P

F32 = jnp.float32
BF16 = jnp.bfloat16
LANES = 128


def split(value):
    high = value.astype(BF16)
    low = (value - high.astype(F32)).astype(BF16)
    return high, low


def shift_rows(value, step, depth):
    rows = value.shape[0]
    place = lax.broadcasted_iota(jnp.int32, value.shape, 0) % depth
    moved = pltpu.roll(value, (-step) % rows, 0)
    inside = (place + step >= 0) & (place + step < depth)
    return jnp.where(inside, moved, 0.0)


def stack_terms(value):
    return jnp.concatenate(split(value), axis=-1)


def products(piece, high, low, dim):
    channels = high.shape[0]

    def dot(left, right):
        return lax.dot_general(
            left, right, (((1,), (dim,)), ((), ())), preferred_element_type=F32
        )

    own_high, own_low = piece[:, :channels], piece[:, channels:]
    return dot(own_high, high) + dot(own_low, high) + dot(own_high, low)


WHOLE = pl.BlockSpec(memory_space=pltpu.VMEM)


def params(mib):
    return pltpu.CompilerParams(vmem_limit_bytes=mib * 1024 * 1024)


def padded_slab(index, span, own, before_x, after_x, before_y, after_y):
    if index == 0:
        middle = before_x[0]
    elif index == span + 1:
        middle = after_x[0]
    else:
        middle = own(index - 1)
    return jnp.concatenate([before_y[index], middle, after_y[index]], axis=0)


def forward_kernel(
    swap_ref,
    inputs_ref,
    filled_ref,
    before_x_ref,
    after_x_ref,
    before_y_ref,
    after_y_ref,
    cot_ref,
    weight_ref,
    up_ref,
    turned_ref,
    right_ref,
    stack_ref,
    acc_ref,
    slab_ref,
):
    step = pl.program_id(0)
    span_x, span_y, depth, channels = inputs_ref.shape
    count, side = span_x * span_y * depth, span_y * depth

    @pl.when(step == 0)
    def _():
        for i in range(span_x + 2):
            slab = padded_slab(
                i,
                span_x,
                lambda x: inputs_ref[x] * filled_ref[x],
                before_x_ref,
                after_x_ref,
                before_y_ref,
                after_y_ref,
            )
            slab_ref[i] = slab
            stack_ref[i] = stack_terms(slab)
        acc_ref[...] = jnp.zeros_like(acc_ref)

    for third in range(3):
        total = acc_ref[third]
        for second in range(3):
            piece = stack_ref[pl.ds(step, span_x), second : second + span_y]
            total += products(
                piece.reshape(count, 2 * channels),
                *split(weight_ref[9 * step + 3 * second + third]),
                0,
            )
        acc_ref[third] = total

    each = -(-(span_x + 2) // 3)
    groups = channels // 16
    for j in range(each):
        i = jnp.minimum(step * each + j, span_x + 1)
        lanes = pl.ds(pl.multiple_of(i * side, LANES), side)
        for second in range(3):
            turn = slab_ref[i, second : second + span_y].reshape(side, channels).T
            high, low = split(turn)
            for m in range(groups):
                at = ((m % 2) * 3 + second) * (channels // 2) + 16 * (m // 2)
                turned_ref[0, at : at + 16, lanes] = high[16 * m : 16 * m + 16]
                turned_ref[1, at : at + 16, lanes] = low[16 * m : 16 * m + 16]

    @pl.when(step == 2)
    def _():
        preact = (
            acc_ref[1] + shift_rows(acc_ref[0], -1, depth) + shift_rows(acc_ref[2], 1, depth)
        )
        sigma = jax.nn.sigmoid(preact)
        cot = cot_ref[...] * filled_ref[...].reshape(count, 1)
        upstream = cot * sigma * (1.0 + preact * (1.0 - sigma))
        up_ref[...] = upstream

        left, right = upstream[:, :LANES], upstream[:, LANES:]
        swap_high, swap_low = swap_ref[0] > 0, swap_ref[1] > 0
        left, right = jnp.where(swap_high, right, left), jnp.where(swap_high, left, right)
        left = jnp.where(swap_low, pltpu.roll(left, 64, 1), left)
        right = jnp.where(swap_low, pltpu.roll(right, 64, 1), right)
        ordered = jnp.concatenate([left, right], axis=1)
        for third in range(3):
            high, low = split(shift_rows(ordered, 1 - third, depth))
            right_ref[third, 0] = high
            right_ref[third, 1] = low


def lines_kernel(inputs_ref, filled_ref, weight_ref, first_ref, last_ref):
    first_ref[...] = inputs_ref[:, 0] * filled_ref[:, 0]
    last = inputs_ref.shape[1] - 1
    last_ref[...] = inputs_ref[:, last] * filled_ref[:, last]


def edge_lines(inputs, filled, taps):
    span_x, span_y, depth, channels = inputs.shape
    line = jax.ShapeDtypeStruct((span_x, depth, channels), F32)
    return pl.pallas_call(
        lines_kernel,
        in_specs=[WHOLE] * 3,
        out_specs=[WHOLE] * 2,
        out_shape=[line] * 2,
        compiler_params=params(4),
        cost_estimate=pl.CostEstimate(
            flops=line.size, bytes_accessed=4 * line.size, transcendentals=0
        ),
    )(inputs, filled, taps)


def forward(swap, inputs, filled, before_x, after_x, before_y, after_y, cot, taps):
    span_x, span_y, depth, channels = inputs.shape
    count = span_x * span_y * depth
    turned = (2, 3 * channels, (span_x + 2) * span_y * depth)
    right = (3, 2, count, channels)
    return pl.pallas_call(
        forward_kernel,
        grid=(3,),
        in_specs=[pl.BlockSpec(memory_space=pltpu.SMEM)]
        + [WHOLE] * 8,
        out_specs=[WHOLE] * 3,
        out_shape=[
            jax.ShapeDtypeStruct((count, channels), F32),
            jax.ShapeDtypeStruct(turned, BF16),
            jax.ShapeDtypeStruct(right, BF16),
        ],
        scratch_shapes=[
            pltpu.VMEM((span_x + 2, span_y + 2, depth, 2 * channels), BF16),
            pltpu.VMEM((3, count, channels), F32),
            pltpu.VMEM((span_x + 2, span_y + 2, depth, channels), F32),
        ],
        compiler_params=params(24),
        cost_estimate=pl.CostEstimate(
            flops=count * channels,
            bytes_accessed=inputs.size,
            transcendentals=count * channels,
        ),
    )(swap, inputs, filled, before_x, after_x, before_y, after_y, cot, taps)


def filter_kernel(part, side, place_ref, turned_ref, right_ref, keep_ref, send_ref, acc_ref):
    count, channels = right_ref.shape[2:]
    low_lanes = lax.broadcasted_iota(jnp.int32, (8, LANES), 1) < 64
    keep_jump, send_jump = place_ref[0, 0], place_ref[1, 0]
    seen = 0
    rows = 3 * (channels // 2)
    base = part * rows
    for third in range(3):
        for first in range(3):
            lanes = slice(first * side, first * side + count)
            high = turned_ref[0, base : base + rows, lanes]
            low = turned_ref[1, base : base + rows, lanes]
            acc_ref[...] = (
                jnp.dot(high, right_ref[third, 0], preferred_element_type=F32)
                + jnp.dot(low, right_ref[third, 0], preferred_element_type=F32)
                + jnp.dot(high, right_ref[third, 1], preferred_element_type=F32)
            )
            for group in range(rows // 16):
                keep_at, send_at = place_ref[0, 1 + seen], place_ref[1, 1 + seen]
                seen += 1
                start = group * 16
                for high_half in range(2):
                    columns = slice(high_half * LANES, (high_half + 1) * LANES)
                    upper = acc_ref[start : start + 8, columns]
                    lower = acc_ref[start + 8 : start + 16, columns]
                    keep_ref[keep_at + high_half * keep_jump] = jnp.where(
                        low_lanes, upper, pltpu.roll(lower, 64, 1)
                    )
                    send_ref[send_at + high_half * send_jump] = jnp.where(
                        low_lanes, pltpu.roll(upper, 64, 1), lower
                    )


def filter_terms(part, place, turned, right, tiles, side):
    count, channels = right.shape[2:]

    def kernel(*refs):
        filter_kernel(part, side, *refs)

    shape = jax.ShapeDtypeStruct((tiles, 8, LANES), F32)
    return pl.pallas_call(
        kernel,
        in_specs=[pl.BlockSpec(memory_space=pltpu.SMEM), WHOLE, WHOLE],
        out_specs=[WHOLE] * 2,
        out_shape=[shape] * 2,
        scratch_shapes=[pltpu.VMEM((3 * channels // 2, channels), F32)],
        compiler_params=params(12),
        cost_estimate=pl.CostEstimate(
            flops=count * channels,
            bytes_accessed=count * channels,
            transcendentals=0,
        ),
    )(place, turned, right)


def unit_tables(channels, size_x):
    groups = channels // 16
    units = 27 * groups // size_x
    tables = []
    for part in range(2):
        order = [
            (first * 9 + second * 3 + third) * groups + m
            for third in range(3)
            for first in range(3)
            for second in range(3)
            for m in range(part, groups, 2)
        ]
        unit = np.array(order, np.int32)
        tables.append((unit // units, unit % units // 2))
    return tables


def data_kernel(
    begin,
    end,
    turn_ref,
    up_ref,
    filled_ref,
    before_x_ref,
    after_x_ref,
    before_y_ref,
    after_y_ref,
    weight_ref,
    out_ref,
    stack_ref,
    acc_ref,
):
    step = pl.program_id(0)
    span_x, span_y, depth, channels = up_ref.shape
    width = end - begin
    count = width * span_y * depth

    @pl.when(step == 0)
    def _():
        for i in range(width + 2):
            stack_ref[i] = stack_terms(
                padded_slab(
                    begin + i,
                    span_x,
                    lambda x: up_ref[x],
                    before_x_ref,
                    after_x_ref,
                    before_y_ref,
                    after_y_ref,
                )
            )
        acc_ref[...] = jnp.zeros_like(acc_ref)

    for third in range(3):
        total = acc_ref[third]
        for second in range(3):
            piece = stack_ref[pl.ds(2 - step, width), 2 - second : 2 - second + span_y]
            total += products(
                piece.reshape(count, 2 * channels),
                *split(weight_ref[9 * step + 3 * second + third]),
                1,
            )
        acc_ref[third] = total

    @pl.when(step == 2)
    def _():
        total = acc_ref[1] + shift_rows(acc_ref[0], 1, depth) + shift_rows(acc_ref[2], -1, depth)
        out_ref[...] = total * filled_ref[begin:end].reshape(count, 1)


def data_grad(turn, up, filled, before_x, after_x, before_y, after_y, taps, begin, end):
    span_x, span_y, depth, channels = up.shape
    width = end - begin
    count = width * span_y * depth

    def kernel(*refs):
        data_kernel(begin, end, *refs)

    return pl.pallas_call(
        kernel,
        grid=(3,),
        in_specs=[pl.BlockSpec(memory_space=pltpu.SMEM)] + [WHOLE] * 7,
        out_specs=WHOLE,
        out_shape=jax.ShapeDtypeStruct((count, channels), F32),
        scratch_shapes=[
            pltpu.VMEM((width + 2, span_y + 2, depth, 2 * channels), BF16),
            pltpu.VMEM((3, count, channels), F32),
        ],
        compiler_params=params(16),
        cost_estimate=pl.CostEstimate(
            flops=count * channels,
            bytes_accessed=count * channels,
            transcendentals=0,
        ),
    )(turn, up, filled, before_x, after_x, before_y, after_y, taps)


def bits_of(size):
    return size.bit_length() - 1


def after(value, *others):
    return lax.optimization_barrier((value, *others))[0]


def neighbours(axis):
    size = lax.axis_size(axis)
    up = [(i, i + 1) for i in range(size - 1)]
    return up, [(j, i) for i, j in up]


def halo_x(first, last):
    up, down = neighbours("gx")
    return lax.ppermute(last, "gx", up), lax.ppermute(first, "gx", down)


def halo_y(first, last, before_x, after_x):
    up, down = neighbours("gy")
    span_y = before_x.shape[1]
    low = jnp.concatenate([before_x[:, 0], first, after_x[:, 0]], axis=0)
    high = jnp.concatenate([before_x[:, span_y - 1], last, after_x[:, span_y - 1]], axis=0)
    got = lax.ppermute(high[:, None], "gy", up), lax.ppermute(low[:, None], "gy", down)
    return got


def flip_pairs(size_x, size_y, flips):
    pairs = []
    for x in range(size_x):
        for y in range(size_y):
            axis, bit = flips[y & 1]
            other = (x ^ (1 << bit), y) if axis == "gx" else (x, y ^ (1 << bit))
            pairs.append((x * size_y + y, other[0] * size_y + other[1]))
    return pairs


def plain_filter_grad(bordered, upstream, span_x, span_y, depth):
    padded = jnp.pad(bordered, ((0, 0), (0, 0), (1, 1), (0, 0)))
    blocks = []
    for first in range(3):
        for second in range(3):
            for third in range(3):
                piece = padded[
                    first : first + span_x, second : second + span_y, third : third + depth
                ].reshape(upstream.shape)
                blocks.append(
                    jnp.dot(
                        piece.T,
                        upstream,
                        precision=lax.Precision.HIGHEST,
                        preferred_element_type=F32,
                    )
                )
    term = jnp.concatenate(blocks, axis=0)
    row_sums = lax.psum_scatter(term, "gx", scatter_dimension=0, tiled=True)
    return lax.psum_scatter(row_sums, "gy", scatter_dimension=1, tiled=True)


def body(inputs, cotangent, weight, occupancy):
    span_x, span_y, depth, channels = inputs.shape
    count = span_x * span_y * depth
    size_x, size_y = lax.axis_size("gx"), lax.axis_size("gy")
    me_x, me_y = lax.axis_index("gx"), lax.axis_index("gy")
    filled = occupancy.astype(F32)[..., None]
    taps = weight.reshape(27, channels, channels)
    cot = cotangent.reshape(count, channels)

    def masked(x, y):
        return inputs[x, y] * filled[x, y]

    every = slice(None)
    last_x, last_y = span_x - 1, span_y - 1
    face, other_face = masked(slice(0, 1), every), masked(slice(last_x, span_x), every)
    before_x, after_x = halo_x(face, other_face)
    taps = after(taps, face, other_face)
    before_y, after_y = halo_y(*edge_lines(inputs, filled, taps), before_x, after_x)
    swap = jnp.stack([(me_y >> 1) & 1, me_y & 1]).astype(jnp.int32)
    upstream, turned, right = forward(
        swap,
        inputs,
        filled,
        before_x,
        after_x,
        before_y.reshape(span_x + 2, 1, depth, channels),
        after_y.reshape(span_x + 2, 1, depth, channels),
        cot,
        taps,
    )
    up = upstream.reshape(inputs.shape)

    def data_halo_x(*others):
        first, last = up[:1], up[last_x:]
        if others:
            first, last, _ = lax.optimization_barrier((first, last, others))
        return first, halo_x(first, last)

    def data_halo_y(sides, *others):
        first, last = up[:, 0], up[:, last_y]
        if others:
            first, last, _ = lax.optimization_barrier((first, last, others))
        return first, halo_y(first, last, *sides)

    def data_piece(turn, sides, ends, begin, end):
        return data_grad(turn, up, filled, *sides, *ends, taps, begin, end)

    middle = span_x // 2
    parts, groups = 2, channels // 16
    if channels // size_y != 64 or 27 * groups % (parts * size_x) or channels != 256:
        own = inputs * filled
        bordered = jnp.concatenate(
            [before_y, jnp.concatenate([before_x, own, after_x], axis=0), after_y], axis=1
        )
        weight_grad = plain_filter_grad(bordered, upstream, span_x, span_y, depth)
        sides = data_halo_x()[1]
        result = data_piece(swap, sides, data_halo_y(sides)[1], 0, span_x)
        return (result.reshape(inputs.shape), weight_grad)

    units = 27 * groups // size_x // parts
    rest = [("gx", b) for b in range(1, bits_of(size_x))]
    x_bit, y_bit = ("gx", 0), ("gy", 1)
    paths = [
        ([x_bit, y_bit] + rest, [y_bit, x_bit] + rest),
        ([y_bit, x_bit] + rest, rest + [x_bit, y_bit]),
    ]
    tiles = 2 * size_x * units
    core = [(i, i ^ 1) for i in range(size_y)]
    tables = []
    for part, (chunk, place) in enumerate(unit_tables(channels, size_x)):
        relative = jnp.asarray(chunk) ^ me_x
        ways = []
        for path in paths[part]:
            at, jump = jnp.zeros_like(relative), 0
            for position, (axis, bit) in enumerate(path):
                worth = 1 << (len(path) - 1 - position)
                if axis == "gx":
                    at = at + ((relative >> bit) & 1) * worth
                else:
                    jump = worth * units
            at = at * units + jnp.asarray(place)
            ways.append(jnp.concatenate([jnp.full((1,), jump, jnp.int32), at]))
        tables.append(jnp.where(me_y & 1, jnp.stack(ways[::-1]), jnp.stack(ways)))
    flips = [list(zip(*path)) for path in paths]
    stages = len(flips[0])

    def terms(part, table):
        keep, send = filter_terms(part, table, turned, right, tiles, span_y * depth)
        return keep, send, lax.ppermute(send, "gy", core)

    def stage(part, index, keep, got):
        half = keep.shape[0] // 2
        send, keep = keep[half:] + got[half:], keep[:half] + got[:half]
        pairs = flip_pairs(size_x, size_y, flips[part][index])
        return keep, send, lax.ppermute(send, ("gx", "gy"), pairs)

    keep_a, send_a, got_a = terms(0, tables[0])
    keep_b, send_b, got_b = terms(1, after(tables[1], send_a))
    keep_a, send_a, got_a = stage(0, 0, after(keep_a, send_b), got_a)
    face, sides = data_halo_x(send_a)
    keep_b, send_b, got_b = stage(1, 0, after(keep_b, face), got_b)
    keep_a, send_a, got_a = stage(0, 1, after(keep_a, send_b), got_a)
    line, ends = data_halo_y(sides, send_a)
    keep_b, send_b, got_b = stage(1, 1, after(keep_b, line), got_b)
    pieces = [data_piece(after(swap, send_b), sides, ends, 0, middle)]
    for index in range(2, stages):
        keep_a, send_a, got_a = stage(0, index, after(keep_a, pieces[-1], send_b), got_a)
        keep_b, send_b, got_b = stage(1, index, after(keep_b, send_a), got_b)
        if index == 2:
            pieces.append(data_piece(after(swap, send_b), sides, ends, middle, span_x))
    sums = [keep_a + got_a, keep_b + got_b]
    both = jnp.stack([s.reshape(units, 8, 2, 64) for s in sums], axis=1)
    weight_grad = both.transpose(0, 1, 3, 2, 4).reshape(units * 32, 64)
    return (jnp.concatenate(pieces, axis=0).reshape(inputs.shape), weight_grad)


def solution(mesh):
    in_specs = (P("gx", "gy", None, None), P("gx", "gy", None, None), P(), P("gx", "gy", None))
    out_specs = (P("gx", "gy", None, None), P("gx", "gy"))
    return jax.shard_map(body, mesh=mesh, in_specs=in_specs, out_specs=out_specs, check_vma=False)
```

```python
import jax
import jax.numpy as jnp
import numpy as np
from jax import lax
from jax.experimental import pallas as pl
from jax.experimental.pallas import tpu as pltpu
from jax.sharding import PartitionSpec as P

F32 = jnp.float32
BF16 = jnp.bfloat16
LANES = 128


def split(value):
    high = value.astype(BF16)
    low = (value - high.astype(F32)).astype(BF16)
    return high, low


def shift_rows(value, step, depth):
    rows = value.shape[0]
    place = lax.broadcasted_iota(jnp.int32, value.shape, 0) % depth
    moved = pltpu.roll(value, (-step) % rows, 0)
    inside = (place + step >= 0) & (place + step < depth)
    return jnp.where(inside, moved, 0.0)


def stack_terms(value):
    return jnp.concatenate(split(value), axis=-1)


def products(piece, high, low, dim):
    channels = high.shape[0]

    def dot(left, right):
        return lax.dot_general(
            left, right, (((1,), (dim,)), ((), ())), preferred_element_type=F32
        )

    own_high, own_low = piece[:, :channels], piece[:, channels:]
    return dot(own_high, high) + dot(own_low, high) + dot(own_high, low)


WHOLE = pl.BlockSpec(memory_space=pltpu.VMEM)


def params(mib):
    return pltpu.CompilerParams(vmem_limit_bytes=mib * 1024 * 1024)


def padded_slab(index, span, own, before_x, after_x, before_y, after_y):
    if index == 0:
        middle = before_x[0]
    elif index == span + 1:
        middle = after_x[0]
    else:
        middle = own(index - 1)
    return jnp.concatenate([before_y[index], middle, after_y[index]], axis=0)


def forward_kernel(
    swap_ref,
    inputs_ref,
    filled_ref,
    before_x_ref,
    after_x_ref,
    before_y_ref,
    after_y_ref,
    cot_ref,
    weight_ref,
    up_ref,
    turned_ref,
    right_ref,
    stack_ref,
    acc_ref,
    slab_ref,
):
    step = pl.program_id(0)
    span_x, span_y, depth, channels = inputs_ref.shape
    count, side = span_x * span_y * depth, span_y * depth

    @pl.when(step == 0)
    def _():
        for i in range(span_x + 2):
            slab = padded_slab(
                i,
                span_x,
                lambda x: inputs_ref[x] * filled_ref[x],
                before_x_ref,
                after_x_ref,
                before_y_ref,
                after_y_ref,
            )
            slab_ref[i] = slab
            stack_ref[i] = stack_terms(slab)
        acc_ref[...] = jnp.zeros_like(acc_ref)

    for third in range(3):
        total = acc_ref[third]
        for second in range(3):
            piece = stack_ref[pl.ds(step, span_x), second : second + span_y]
            total += products(
                piece.reshape(count, 2 * channels),
                *split(weight_ref[9 * step + 3 * second + third]),
                0,
            )
        acc_ref[third] = total

    each = -(-(span_x + 2) // 3)
    groups = channels // 16
    for j in range(each):
        i = jnp.minimum(step * each + j, span_x + 1)
        lanes = pl.ds(pl.multiple_of(i * side, LANES), side)
        for second in range(3):
            turn = slab_ref[i, second : second + span_y].reshape(side, channels).T
            high, low = split(turn)
            for m in range(groups):
                at = ((m % 2) * 3 + second) * (channels // 2) + 16 * (m // 2)
                turned_ref[0, at : at + 16, lanes] = high[16 * m : 16 * m + 16]
                turned_ref[1, at : at + 16, lanes] = low[16 * m : 16 * m + 16]

    @pl.when(step == 2)
    def _():
        preact = (
            acc_ref[1] + shift_rows(acc_ref[0], -1, depth) + shift_rows(acc_ref[2], 1, depth)
        )
        sigma = jax.nn.sigmoid(preact)
        cot = cot_ref[...] * filled_ref[...].reshape(count, 1)
        upstream = cot * sigma * (1.0 + preact * (1.0 - sigma))
        up_ref[...] = upstream

        left, right = upstream[:, :LANES], upstream[:, LANES:]
        swap_high, swap_low = swap_ref[0] > 0, swap_ref[1] > 0
        left, right = jnp.where(swap_high, right, left), jnp.where(swap_high, left, right)
        left = jnp.where(swap_low, pltpu.roll(left, 64, 1), left)
        right = jnp.where(swap_low, pltpu.roll(right, 64, 1), right)
        ordered = jnp.concatenate([left, right], axis=1)
        for third in range(3):
            high, low = split(shift_rows(ordered, 1 - third, depth))
            right_ref[third, 0] = high
            right_ref[third, 1] = low


def lines_kernel(inputs_ref, filled_ref, weight_ref, first_ref, last_ref):
    first_ref[...] = inputs_ref[:, 0] * filled_ref[:, 0]
    last = inputs_ref.shape[1] - 1
    last_ref[...] = inputs_ref[:, last] * filled_ref[:, last]


def edge_lines(inputs, filled, taps):
    span_x, span_y, depth, channels = inputs.shape
    line = jax.ShapeDtypeStruct((span_x, depth, channels), F32)
    return pl.pallas_call(
        lines_kernel,
        in_specs=[WHOLE] * 3,
        out_specs=[WHOLE] * 2,
        out_shape=[line] * 2,
        compiler_params=params(4),
        cost_estimate=pl.CostEstimate(
            flops=line.size, bytes_accessed=4 * line.size, transcendentals=0
        ),
    )(inputs, filled, taps)


def forward(swap, inputs, filled, before_x, after_x, before_y, after_y, cot, taps):
    span_x, span_y, depth, channels = inputs.shape
    count = span_x * span_y * depth
    turned = (2, 3 * channels, (span_x + 2) * span_y * depth)
    right = (3, 2, count, channels)
    return pl.pallas_call(
        forward_kernel,
        grid=(3,),
        in_specs=[pl.BlockSpec(memory_space=pltpu.SMEM)]
        + [WHOLE] * 8,
        out_specs=[WHOLE] * 3,
        out_shape=[
            jax.ShapeDtypeStruct((count, channels), F32),
            jax.ShapeDtypeStruct(turned, BF16),
            jax.ShapeDtypeStruct(right, BF16),
        ],
        scratch_shapes=[
            pltpu.VMEM((span_x + 2, span_y + 2, depth, 2 * channels), BF16),
            pltpu.VMEM((3, count, channels), F32),
            pltpu.VMEM((span_x + 2, span_y + 2, depth, channels), F32),
        ],
        compiler_params=params(24),
        cost_estimate=pl.CostEstimate(
            flops=count * channels,
            bytes_accessed=inputs.size,
            transcendentals=count * channels,
        ),
    )(swap, inputs, filled, before_x, after_x, before_y, after_y, cot, taps)


def filter_kernel(part, side, place_ref, turned_ref, right_ref, keep_ref, send_ref, acc_ref):
    count, channels = right_ref.shape[2:]
    low_lanes = lax.broadcasted_iota(jnp.int32, (8, LANES), 1) < 64
    keep_jump, send_jump = place_ref[0, 0], place_ref[1, 0]
    seen = 0
    rows = 3 * (channels // 2)
    base = part * rows
    for third in range(3):
        for first in range(3):
            lanes = slice(first * side, first * side + count)
            high = turned_ref[0, base : base + rows, lanes]
            low = turned_ref[1, base : base + rows, lanes]
            acc_ref[...] = (
                jnp.dot(high, right_ref[third, 0], preferred_element_type=F32)
                + jnp.dot(low, right_ref[third, 0], preferred_element_type=F32)
                + jnp.dot(high, right_ref[third, 1], preferred_element_type=F32)
            )
            for group in range(rows // 16):
                keep_at, send_at = place_ref[0, 1 + seen], place_ref[1, 1 + seen]
                seen += 1
                start = group * 16
                for high_half in range(2):
                    columns = slice(high_half * LANES, (high_half + 1) * LANES)
                    upper = acc_ref[start : start + 8, columns]
                    lower = acc_ref[start + 8 : start + 16, columns]
                    keep_ref[keep_at + high_half * keep_jump] = jnp.where(
                        low_lanes, upper, pltpu.roll(lower, 64, 1)
                    )
                    send_ref[send_at + high_half * send_jump] = jnp.where(
                        low_lanes, pltpu.roll(upper, 64, 1), lower
                    )


def filter_terms(part, place, turned, right, tiles, side):
    count, channels = right.shape[2:]

    def kernel(*refs):
        filter_kernel(part, side, *refs)

    shape = jax.ShapeDtypeStruct((tiles, 8, LANES), F32)
    return pl.pallas_call(
        kernel,
        in_specs=[pl.BlockSpec(memory_space=pltpu.SMEM), WHOLE, WHOLE],
        out_specs=[WHOLE] * 2,
        out_shape=[shape] * 2,
        scratch_shapes=[pltpu.VMEM((3 * channels // 2, channels), F32)],
        compiler_params=params(12),
        cost_estimate=pl.CostEstimate(
            flops=count * channels,
            bytes_accessed=count * channels,
            transcendentals=0,
        ),
    )(place, turned, right)


def unit_tables(channels, size_x):
    groups = channels // 16
    units = 27 * groups // size_x
    tables = []
    for part in range(2):
        order = [
            (first * 9 + second * 3 + third) * groups + m
            for third in range(3)
            for first in range(3)
            for second in range(3)
            for m in range(part, groups, 2)
        ]
        unit = np.array(order, np.int32)
        tables.append((unit // units, unit % units // 2))
    return tables


def data_kernel(
    begin,
    end,
    turn_ref,
    up_ref,
    filled_ref,
    before_x_ref,
    after_x_ref,
    before_y_ref,
    after_y_ref,
    weight_ref,
    out_ref,
    stack_ref,
    acc_ref,
):
    step = pl.program_id(0)
    span_x, span_y, depth, channels = up_ref.shape
    width = end - begin
    count = width * span_y * depth

    @pl.when(step == 0)
    def _():
        for i in range(width + 2):
            stack_ref[i] = stack_terms(
                padded_slab(
                    begin + i,
                    span_x,
                    lambda x: up_ref[x],
                    before_x_ref,
                    after_x_ref,
                    before_y_ref,
                    after_y_ref,
                )
            )
        acc_ref[...] = jnp.zeros_like(acc_ref)

    for third in range(3):
        total = acc_ref[third]
        for second in range(3):
            piece = stack_ref[pl.ds(2 - step, width), 2 - second : 2 - second + span_y]
            total += products(
                piece.reshape(count, 2 * channels),
                *split(weight_ref[9 * step + 3 * second + third]),
                1,
            )
        acc_ref[third] = total

    @pl.when(step == 2)
    def _():
        total = acc_ref[1] + shift_rows(acc_ref[0], 1, depth) + shift_rows(acc_ref[2], -1, depth)
        out_ref[...] = total * filled_ref[begin:end].reshape(count, 1)


def data_grad(turn, up, filled, before_x, after_x, before_y, after_y, taps, begin, end):
    span_x, span_y, depth, channels = up.shape
    width = end - begin
    count = width * span_y * depth

    def kernel(*refs):
        data_kernel(begin, end, *refs)

    return pl.pallas_call(
        kernel,
        grid=(3,),
        in_specs=[pl.BlockSpec(memory_space=pltpu.SMEM)] + [WHOLE] * 7,
        out_specs=WHOLE,
        out_shape=jax.ShapeDtypeStruct((count, channels), F32),
        scratch_shapes=[
            pltpu.VMEM((width + 2, span_y + 2, depth, 2 * channels), BF16),
            pltpu.VMEM((3, count, channels), F32),
        ],
        compiler_params=params(16),
        cost_estimate=pl.CostEstimate(
            flops=count * channels,
            bytes_accessed=count * channels,
            transcendentals=0,
        ),
    )(turn, up, filled, before_x, after_x, before_y, after_y, taps)


def bits_of(size):
    return size.bit_length() - 1


def after(value, *others):
    return lax.optimization_barrier((value, *others))[0]


def neighbours(axis):
    size = lax.axis_size(axis)
    up = [(i, i + 1) for i in range(size - 1)]
    return up, [(j, i) for i, j in up]


def halo_x(first, last):
    up, down = neighbours("gx")
    return lax.ppermute(last, "gx", up), lax.ppermute(first, "gx", down)


def halo_y(first, last, before_x, after_x):
    up, down = neighbours("gy")
    span_y = before_x.shape[1]
    low = jnp.concatenate([before_x[:, 0], first, after_x[:, 0]], axis=0)
    high = jnp.concatenate([before_x[:, span_y - 1], last, after_x[:, span_y - 1]], axis=0)
    got = lax.ppermute(high[:, None], "gy", up), lax.ppermute(low[:, None], "gy", down)
    return got


def flip_pairs(size_x, size_y, flips):
    pairs = []
    for x in range(size_x):
        for y in range(size_y):
            axis, bit = flips[y & 1]
            other = (x ^ (1 << bit), y) if axis == "gx" else (x, y ^ (1 << bit))
            pairs.append((x * size_y + y, other[0] * size_y + other[1]))
    return pairs


def plain_filter_grad(bordered, upstream, span_x, span_y, depth):
    padded = jnp.pad(bordered, ((0, 0), (0, 0), (1, 1), (0, 0)))
    blocks = []
    for first in range(3):
        for second in range(3):
            for third in range(3):
                piece = padded[
                    first : first + span_x, second : second + span_y, third : third + depth
                ].reshape(upstream.shape)
                blocks.append(
                    jnp.dot(
                        piece.T,
                        upstream,
                        precision=lax.Precision.HIGHEST,
                        preferred_element_type=F32,
                    )
                )
    term = jnp.concatenate(blocks, axis=0)
    row_sums = lax.psum_scatter(term, "gx", scatter_dimension=0, tiled=True)
    return lax.psum_scatter(row_sums, "gy", scatter_dimension=1, tiled=True)


def body(inputs, cotangent, weight, occupancy):
    span_x, span_y, depth, channels = inputs.shape
    count = span_x * span_y * depth
    size_x, size_y = lax.axis_size("gx"), lax.axis_size("gy")
    me_x, me_y = lax.axis_index("gx"), lax.axis_index("gy")
    filled = occupancy.astype(F32)[..., None]
    taps = weight.reshape(27, channels, channels)
    cot = cotangent.reshape(count, channels)

    def masked(x, y):
        return inputs[x, y] * filled[x, y]

    every = slice(None)
    last_x, last_y = span_x - 1, span_y - 1
    face, other_face = masked(slice(0, 1), every), masked(slice(last_x, span_x), every)
    before_x, after_x = halo_x(face, other_face)
    taps = after(taps, face, other_face)
    before_y, after_y = halo_y(*edge_lines(inputs, filled, taps), before_x, after_x)
    swap = jnp.stack([(me_y >> 1) & 1, me_y & 1]).astype(jnp.int32)
    upstream, turned, right = forward(
        swap,
        inputs,
        filled,
        before_x,
        after_x,
        before_y.reshape(span_x + 2, 1, depth, channels),
        after_y.reshape(span_x + 2, 1, depth, channels),
        cot,
        taps,
    )
    up = upstream.reshape(inputs.shape)

    def data_halo_x(*others):
        first, last = up[:1], up[last_x:]
        if others:
            first, last, _ = lax.optimization_barrier((first, last, others))
        return first, halo_x(first, last)

    def data_halo_y(sides, *others):
        first, last = up[:, 0], up[:, last_y]
        if others:
            first, last, _ = lax.optimization_barrier((first, last, others))
        return first, halo_y(first, last, *sides)

    def data_piece(turn, sides, ends, begin, end):
        return data_grad(turn, up, filled, *sides, *ends, taps, begin, end)

    third = -(-span_x // 3)
    cuts = (third, 2 * third, span_x)
    parts, groups = 2, channels // 16
    tiled = channels == 256 and size_y == 4 and 27 * groups % (parts * size_x) == 0
    if not tiled or size_x < 8 or size_x & (size_x - 1):
        own = inputs * filled
        bordered = jnp.concatenate(
            [before_y, jnp.concatenate([before_x, own, after_x], axis=0), after_y], axis=1
        )
        weight_grad = plain_filter_grad(bordered, upstream, span_x, span_y, depth)
        sides = data_halo_x()[1]
        result = data_piece(swap, sides, data_halo_y(sides)[1], 0, span_x)
        return (result.reshape(inputs.shape), weight_grad)

    units = 27 * groups // size_x // parts
    rest = [("gx", b) for b in range(1, bits_of(size_x))]
    x_bit, y_bit = ("gx", 0), ("gy", 1)
    paths = [
        ([x_bit, y_bit] + rest, [y_bit, x_bit] + rest),
        ([y_bit, x_bit] + rest, rest + [x_bit, y_bit]),
    ]
    tiles = 2 * size_x * units
    core = [(i, i ^ 1) for i in range(size_y)]
    tables = []
    for part, (chunk, place) in enumerate(unit_tables(channels, size_x)):
        relative = jnp.asarray(chunk) ^ me_x
        ways = []
        for path in paths[part]:
            at, jump = jnp.zeros_like(relative), 0
            for position, (axis, bit) in enumerate(path):
                worth = 1 << (len(path) - 1 - position)
                if axis == "gx":
                    at = at + ((relative >> bit) & 1) * worth
                else:
                    jump = worth * units
            at = at * units + jnp.asarray(place)
            ways.append(jnp.concatenate([jnp.full((1,), jump, jnp.int32), at]))
        tables.append(jnp.where(me_y & 1, jnp.stack(ways[::-1]), jnp.stack(ways)))
    flips = [list(zip(*path)) for path in paths]
    stages = len(flips[0])

    def terms(part, table):
        keep, send = filter_terms(part, table, turned, right, tiles, span_y * depth)
        return keep, send, lax.ppermute(send, "gy", core)

    def stage(part, index, keep, got):
        half = keep.shape[0] // 2
        send, keep = keep[half:] + got[half:], keep[:half] + got[:half]
        pairs = flip_pairs(size_x, size_y, flips[part][index])
        return keep, send, lax.ppermute(send, ("gx", "gy"), pairs)

    keep_a, send_a, got_a = terms(0, tables[0])
    keep_b, send_b, got_b = terms(1, after(tables[1], send_a))
    keep_a, send_a, got_a = stage(0, 0, after(keep_a, send_b), got_a)
    face, sides = data_halo_x(send_a)
    keep_b, send_b, got_b = stage(1, 0, after(keep_b, face), got_b)
    keep_a, send_a, got_a = stage(0, 1, after(keep_a, send_b), got_a)
    line, ends = data_halo_y(sides, send_a)
    keep_b, send_b, got_b = stage(1, 1, after(keep_b, line), got_b)
    pieces = [data_piece(after(swap, send_b), sides, ends, 0, cuts[0])]
    for index in range(2, stages):
        keep_a, send_a, got_a = stage(0, index, after(keep_a, pieces[-1], send_b), got_a)
        keep_b, send_b, got_b = stage(1, index, after(keep_b, send_a), got_b)
        if index < 4:
            begin, end = cuts[index - 2 : index]
            pieces.append(data_piece(after(swap, send_b), sides, ends, begin, end))
    sums = [after(keep_a, pieces[-1]) + got_a, after(keep_b, pieces[-1]) + got_b]
    both = jnp.stack([s.reshape(units, 8, 2, 64) for s in sums], axis=1)
    weight_grad = both.transpose(0, 1, 3, 2, 4).reshape(units * 32, 64)
    return (jnp.concatenate(pieces, axis=0).reshape(inputs.shape), weight_grad)


def solution(mesh):
    in_specs = (P("gx", "gy", None, None), P("gx", "gy", None, None), P(), P("gx", "gy", None))
    out_specs = (P("gx", "gy", None, None), P("gx", "gy"))
    return jax.shard_map(body, mesh=mesh, in_specs=in_specs, out_specs=out_specs, check_vma=False)
```

```python
import jax
import jax.numpy as jnp
import numpy as np
from jax import lax
from jax.experimental import pallas as pl
from jax.experimental.pallas import tpu as pltpu
from jax.sharding import PartitionSpec as P

F32 = jnp.float32
BF16 = jnp.bfloat16
LANES = 128


def split(value):
    high = value.astype(BF16)
    low = (value - high.astype(F32)).astype(BF16)
    return high, low


def shift_rows(value, step, depth):
    rows = value.shape[0]
    place = lax.broadcasted_iota(jnp.int32, value.shape, 0) % depth
    moved = pltpu.roll(value, (-step) % rows, 0)
    inside = (place + step >= 0) & (place + step < depth)
    return jnp.where(inside, moved, 0.0)


def stack_terms(value):
    return jnp.concatenate(split(value), axis=-1)


def products(piece, high, low, dim):
    channels = high.shape[0]

    def dot(left, right):
        return lax.dot_general(
            left, right, (((1,), (dim,)), ((), ())), preferred_element_type=F32
        )

    own_high, own_low = piece[:, :channels], piece[:, channels:]
    return dot(own_high, high) + dot(own_low, high) + dot(own_high, low)


WHOLE = pl.BlockSpec(memory_space=pltpu.VMEM)


def params(mib):
    return pltpu.CompilerParams(vmem_limit_bytes=mib * 1024 * 1024)


def padded_slab(index, span, own, before_x, after_x, before_y, after_y):
    if index == 0:
        middle = before_x[0]
    elif index == span + 1:
        middle = after_x[0]
    else:
        middle = own(index - 1)
    return jnp.concatenate([before_y[index], middle, after_y[index]], axis=0)


def forward_kernel(
    swap_ref,
    inputs_ref,
    filled_ref,
    before_x_ref,
    after_x_ref,
    before_y_ref,
    after_y_ref,
    cot_ref,
    weight_ref,
    up_ref,
    turned_ref,
    right_ref,
    stack_ref,
    acc_ref,
    slab_ref,
):
    step = pl.program_id(0)
    span_x, span_y, depth, channels = inputs_ref.shape
    count, side = span_x * span_y * depth, span_y * depth

    @pl.when(step == 0)
    def _():
        for i in range(span_x + 2):
            slab = padded_slab(
                i,
                span_x,
                lambda x: inputs_ref[x] * filled_ref[x],
                before_x_ref,
                after_x_ref,
                before_y_ref,
                after_y_ref,
            )
            slab_ref[i] = slab
            stack_ref[i] = stack_terms(slab)
        acc_ref[...] = jnp.zeros_like(acc_ref)

    for third in range(3):
        total = acc_ref[third]
        for second in range(3):
            piece = stack_ref[pl.ds(step, span_x), second : second + span_y]
            total += products(
                piece.reshape(count, 2 * channels),
                *split(weight_ref[9 * step + 3 * second + third]),
                0,
            )
        acc_ref[third] = total

    each = -(-(span_x + 2) // 3)
    groups = channels // 16
    for j in range(each):
        i = jnp.minimum(step * each + j, span_x + 1)
        lanes = pl.ds(pl.multiple_of(i * side, LANES), side)
        for second in range(3):
            turn = slab_ref[i, second : second + span_y].reshape(side, channels).T
            high, low = split(turn)
            for m in range(groups):
                at = ((m % 2) * 3 + second) * (channels // 2) + 16 * (m // 2)
                turned_ref[0, at : at + 16, lanes] = high[16 * m : 16 * m + 16]
                turned_ref[1, at : at + 16, lanes] = low[16 * m : 16 * m + 16]

    @pl.when(step == 2)
    def _():
        preact = (
            acc_ref[1] + shift_rows(acc_ref[0], -1, depth) + shift_rows(acc_ref[2], 1, depth)
        )
        sigma = jax.nn.sigmoid(preact)
        cot = cot_ref[...] * filled_ref[...].reshape(count, 1)
        upstream = cot * sigma * (1.0 + preact * (1.0 - sigma))
        up_ref[...] = upstream

        left, right = upstream[:, :LANES], upstream[:, LANES:]
        swap_high, swap_low = swap_ref[0] > 0, swap_ref[1] > 0
        left, right = jnp.where(swap_high, right, left), jnp.where(swap_high, left, right)
        left = jnp.where(swap_low, pltpu.roll(left, 64, 1), left)
        right = jnp.where(swap_low, pltpu.roll(right, 64, 1), right)
        ordered = jnp.concatenate([left, right], axis=1)
        for third in range(3):
            high, low = split(shift_rows(ordered, 1 - third, depth))
            right_ref[third, 0] = high
            right_ref[third, 1] = low


def lines_kernel(inputs_ref, filled_ref, weight_ref, first_ref, last_ref):
    first_ref[...] = inputs_ref[:, 0] * filled_ref[:, 0]
    last = inputs_ref.shape[1] - 1
    last_ref[...] = inputs_ref[:, last] * filled_ref[:, last]


def edge_lines(inputs, filled, taps):
    span_x, span_y, depth, channels = inputs.shape
    line = jax.ShapeDtypeStruct((span_x, depth, channels), F32)
    return pl.pallas_call(
        lines_kernel,
        in_specs=[WHOLE] * 3,
        out_specs=[WHOLE] * 2,
        out_shape=[line] * 2,
        compiler_params=params(4),
        cost_estimate=pl.CostEstimate(
            flops=line.size, bytes_accessed=4 * line.size, transcendentals=0
        ),
    )(inputs, filled, taps)


def forward(swap, inputs, filled, before_x, after_x, before_y, after_y, cot, taps):
    span_x, span_y, depth, channels = inputs.shape
    count = span_x * span_y * depth
    turned = (2, 3 * channels, (span_x + 2) * span_y * depth)
    right = (3, 2, count, channels)
    return pl.pallas_call(
        forward_kernel,
        grid=(3,),
        in_specs=[pl.BlockSpec(memory_space=pltpu.SMEM)]
        + [WHOLE] * 8,
        out_specs=[WHOLE] * 3,
        out_shape=[
            jax.ShapeDtypeStruct((count, channels), F32),
            jax.ShapeDtypeStruct(turned, BF16),
            jax.ShapeDtypeStruct(right, BF16),
        ],
        scratch_shapes=[
            pltpu.VMEM((span_x + 2, span_y + 2, depth, 2 * channels), BF16),
            pltpu.VMEM((3, count, channels), F32),
            pltpu.VMEM((span_x + 2, span_y + 2, depth, channels), F32),
        ],
        compiler_params=params(24),
        cost_estimate=pl.CostEstimate(
            flops=count * channels,
            bytes_accessed=inputs.size,
            transcendentals=count * channels,
        ),
    )(swap, inputs, filled, before_x, after_x, before_y, after_y, cot, taps)


def filter_kernel(part, side, place_ref, turned_ref, right_ref, keep_ref, send_ref, acc_ref):
    count, channels = right_ref.shape[2:]
    low_lanes = lax.broadcasted_iota(jnp.int32, (8, LANES), 1) < 64
    keep_jump, send_jump = place_ref[0, 0], place_ref[1, 0]
    seen = 0
    rows = 3 * (channels // 2)
    base = part * rows
    for third in range(3):
        for first in range(3):
            lanes = slice(first * side, first * side + count)
            high = turned_ref[0, base : base + rows, lanes]
            low = turned_ref[1, base : base + rows, lanes]
            acc_ref[...] = (
                jnp.dot(high, right_ref[third, 0], preferred_element_type=F32)
                + jnp.dot(low, right_ref[third, 0], preferred_element_type=F32)
                + jnp.dot(high, right_ref[third, 1], preferred_element_type=F32)
            )
            for group in range(rows // 16):
                keep_at, send_at = place_ref[0, 1 + seen], place_ref[1, 1 + seen]
                seen += 1
                start = group * 16
                for high_half in range(2):
                    columns = slice(high_half * LANES, (high_half + 1) * LANES)
                    upper = acc_ref[start : start + 8, columns]
                    lower = acc_ref[start + 8 : start + 16, columns]
                    keep_ref[keep_at + high_half * keep_jump] = jnp.where(
                        low_lanes, upper, pltpu.roll(lower, 64, 1)
                    )
                    send_ref[send_at + high_half * send_jump] = jnp.where(
                        low_lanes, pltpu.roll(upper, 64, 1), lower
                    )


def filter_terms(part, place, turned, right, tiles, side):
    count, channels = right.shape[2:]

    def kernel(*refs):
        filter_kernel(part, side, *refs)

    shape = jax.ShapeDtypeStruct((tiles, 8, LANES), F32)
    return pl.pallas_call(
        kernel,
        in_specs=[pl.BlockSpec(memory_space=pltpu.SMEM), WHOLE, WHOLE],
        out_specs=[WHOLE] * 2,
        out_shape=[shape] * 2,
        scratch_shapes=[pltpu.VMEM((3 * channels // 2, channels), F32)],
        compiler_params=params(12),
        cost_estimate=pl.CostEstimate(
            flops=count * channels,
            bytes_accessed=count * channels,
            transcendentals=0,
        ),
    )(place, turned, right)


def unit_tables(channels, size_x):
    groups = channels // 16
    units = 27 * groups // size_x
    tables = []
    for part in range(2):
        order = [
            (first * 9 + second * 3 + third) * groups + m
            for third in range(3)
            for first in range(3)
            for second in range(3)
            for m in range(part, groups, 2)
        ]
        unit = np.array(order, np.int32)
        tables.append((unit // units, unit % units // 2))
    return tables


def data_kernel(
    begin,
    end,
    turn_ref,
    up_ref,
    filled_ref,
    before_x_ref,
    after_x_ref,
    before_y_ref,
    after_y_ref,
    weight_ref,
    out_ref,
    stack_ref,
    acc_ref,
):
    step = pl.program_id(0)
    span_x, span_y, depth, channels = up_ref.shape
    width = end - begin
    count = width * span_y * depth

    @pl.when(step == 0)
    def _():
        for i in range(width + 2):
            stack_ref[i] = stack_terms(
                padded_slab(
                    begin + i,
                    span_x,
                    lambda x: up_ref[x],
                    before_x_ref,
                    after_x_ref,
                    before_y_ref,
                    after_y_ref,
                )
            )
        acc_ref[...] = jnp.zeros_like(acc_ref)

    for third in range(3):
        total = acc_ref[third]
        for second in range(3):
            piece = stack_ref[pl.ds(2 - step, width), 2 - second : 2 - second + span_y]
            total += products(
                piece.reshape(count, 2 * channels),
                *split(weight_ref[9 * step + 3 * second + third]),
                1,
            )
        acc_ref[third] = total

    @pl.when(step == 2)
    def _():
        total = acc_ref[1] + shift_rows(acc_ref[0], 1, depth) + shift_rows(acc_ref[2], -1, depth)
        out_ref[...] = total * filled_ref[begin:end].reshape(count, 1)


def data_grad(turn, up, filled, before_x, after_x, before_y, after_y, taps, begin, end):
    span_x, span_y, depth, channels = up.shape
    width = end - begin
    count = width * span_y * depth

    def kernel(*refs):
        data_kernel(begin, end, *refs)

    return pl.pallas_call(
        kernel,
        grid=(3,),
        in_specs=[pl.BlockSpec(memory_space=pltpu.SMEM)] + [WHOLE] * 7,
        out_specs=WHOLE,
        out_shape=jax.ShapeDtypeStruct((count, channels), F32),
        scratch_shapes=[
            pltpu.VMEM((width + 2, span_y + 2, depth, 2 * channels), BF16),
            pltpu.VMEM((3, count, channels), F32),
        ],
        compiler_params=params(16),
        cost_estimate=pl.CostEstimate(
            flops=count * channels,
            bytes_accessed=count * channels,
            transcendentals=0,
        ),
    )(turn, up, filled, before_x, after_x, before_y, after_y, taps)


def bits_of(size):
    return size.bit_length() - 1


def after(value, *others):
    return lax.optimization_barrier((value, *others))[0]


def neighbours(axis):
    size = lax.axis_size(axis)
    up = [(i, i + 1) for i in range(size - 1)]
    return up, [(j, i) for i, j in up]


def halo_x(first, last):
    up, down = neighbours("gx")
    return lax.ppermute(last, "gx", up), lax.ppermute(first, "gx", down)


def halo_y(first, last, before_x, after_x):
    up, down = neighbours("gy")
    span_y = before_x.shape[1]
    low = jnp.concatenate([before_x[:, 0], first, after_x[:, 0]], axis=0)
    high = jnp.concatenate([before_x[:, span_y - 1], last, after_x[:, span_y - 1]], axis=0)
    got = lax.ppermute(high[:, None], "gy", up), lax.ppermute(low[:, None], "gy", down)
    return got


def flip_pairs(size_x, size_y, flips):
    pairs = []
    for x in range(size_x):
        for y in range(size_y):
            axis, bit = flips[y & 1]
            other = (x ^ (1 << bit), y) if axis == "gx" else (x, y ^ (1 << bit))
            pairs.append((x * size_y + y, other[0] * size_y + other[1]))
    return pairs


def plain_filter_grad(bordered, upstream, span_x, span_y, depth):
    padded = jnp.pad(bordered, ((0, 0), (0, 0), (1, 1), (0, 0)))
    blocks = []
    for first in range(3):
        for second in range(3):
            for third in range(3):
                piece = padded[
                    first : first + span_x, second : second + span_y, third : third + depth
                ].reshape(upstream.shape)
                blocks.append(
                    jnp.dot(
                        piece.T,
                        upstream,
                        precision=lax.Precision.HIGHEST,
                        preferred_element_type=F32,
                    )
                )
    term = jnp.concatenate(blocks, axis=0)
    row_sums = lax.psum_scatter(term, "gx", scatter_dimension=0, tiled=True)
    return lax.psum_scatter(row_sums, "gy", scatter_dimension=1, tiled=True)


def body(inputs, cotangent, weight, occupancy):
    span_x, span_y, depth, channels = inputs.shape
    count = span_x * span_y * depth
    size_x, size_y = lax.axis_size("gx"), lax.axis_size("gy")
    me_x, me_y = lax.axis_index("gx"), lax.axis_index("gy")
    filled = occupancy.astype(F32)[..., None]
    taps = weight.reshape(27, channels, channels)
    cot = cotangent.reshape(count, channels)

    def masked(x, y):
        return inputs[x, y] * filled[x, y]

    every = slice(None)
    last_x, last_y = span_x - 1, span_y - 1
    face, other_face = masked(slice(0, 1), every), masked(slice(last_x, span_x), every)
    before_x, after_x = halo_x(face, other_face)
    taps = after(taps, face, other_face)
    before_y, after_y = halo_y(*edge_lines(inputs, filled, taps), before_x, after_x)
    swap = jnp.stack([(me_y >> 1) & 1, me_y & 1]).astype(jnp.int32)
    upstream, turned, right = forward(
        swap,
        inputs,
        filled,
        before_x,
        after_x,
        before_y.reshape(span_x + 2, 1, depth, channels),
        after_y.reshape(span_x + 2, 1, depth, channels),
        cot,
        taps,
    )
    up = upstream.reshape(inputs.shape)

    def data_halo_x(*others):
        first, last = up[:1], up[last_x:]
        if others:
            first, last, _ = lax.optimization_barrier((first, last, others))
        return first, halo_x(first, last)

    def data_halo_y(sides, *others):
        first, last = up[:, 0], up[:, last_y]
        if others:
            first, last, _ = lax.optimization_barrier((first, last, others))
        return first, halo_y(first, last, *sides)

    def data_piece(turn, sides, ends, begin, end):
        return data_grad(turn, up, filled, *sides, *ends, taps, begin, end)

    third = -(-span_x // 3)
    cuts = (third, 2 * third, span_x)
    parts, groups = 2, channels // 16
    tiled = channels == 256 and size_y == 4 and 27 * groups % (parts * size_x) == 0
    if not tiled or size_x < 8 or size_x & (size_x - 1):
        own = inputs * filled
        bordered = jnp.concatenate(
            [before_y, jnp.concatenate([before_x, own, after_x], axis=0), after_y], axis=1
        )
        weight_grad = plain_filter_grad(bordered, upstream, span_x, span_y, depth)
        sides = data_halo_x()[1]
        result = data_piece(swap, sides, data_halo_y(sides)[1], 0, span_x)
        return (result.reshape(inputs.shape), weight_grad)

    units = 27 * groups // size_x // parts
    rest = [("gx", b) for b in range(1, bits_of(size_x))]
    x_bit, y_bit = ("gx", 0), ("gy", 1)
    paths = [
        ([x_bit, y_bit] + rest, [y_bit, x_bit] + rest),
        ([y_bit, x_bit] + rest, rest + [x_bit, y_bit]),
    ]
    tiles = 2 * size_x * units
    core = [(i, i ^ 1) for i in range(size_y)]
    tables = []
    for part, (chunk, place) in enumerate(unit_tables(channels, size_x)):
        relative = jnp.asarray(chunk) ^ me_x
        ways = []
        for path in paths[part]:
            at, jump = jnp.zeros_like(relative), 0
            for position, (axis, bit) in enumerate(path):
                worth = 1 << (len(path) - 1 - position)
                if axis == "gx":
                    at = at + ((relative >> bit) & 1) * worth
                else:
                    jump = worth * units
            at = at * units + jnp.asarray(place)
            ways.append(jnp.concatenate([jnp.full((1,), jump, jnp.int32), at]))
        tables.append(jnp.where(me_y & 1, jnp.stack(ways[::-1]), jnp.stack(ways)))
    flips = [list(zip(*path)) for path in paths]
    stages = len(flips[0])

    def terms(part, table):
        keep, send = filter_terms(part, table, turned, right, tiles, span_y * depth)
        return keep, send, lax.ppermute(send, "gy", core)

    def stage(part, index, keep, got):
        half = keep.shape[0] // 2
        send, keep = keep[half:] + got[half:], keep[:half] + got[:half]
        pairs = flip_pairs(size_x, size_y, flips[part][index])
        return keep, send, lax.ppermute(send, ("gx", "gy"), pairs)

    keep_a, send_a, got_a = terms(0, tables[0])
    keep_a, send_a, got_a = stage(0, 0, keep_a, got_a)
    face, sides = data_halo_x(send_a)
    keep_b, send_b, got_b = terms(1, after(tables[1], send_a, face))
    keep_a, send_a, got_a = stage(0, 1, after(keep_a, send_b), got_a)
    keep_b, send_b, got_b = stage(1, 0, after(keep_b, send_a), got_b)
    _, ends = data_halo_y(sides, send_b)
    pieces = [data_piece(after(swap, send_b), sides, ends, 0, cuts[0])]
    keep_b, send_b, got_b = stage(1, 1, after(keep_b, pieces[0]), got_b)
    for index in range(2, stages):
        keep_a, send_a, got_a = stage(0, index, after(keep_a, pieces[-1], send_b), got_a)
        keep_b, send_b, got_b = stage(1, index, after(keep_b, send_a), got_b)
        if index < 4:
            begin, end = cuts[index - 2 : index]
            pieces.append(data_piece(after(swap, send_b), sides, ends, begin, end))
    sums = [after(keep_a, pieces[-1]) + got_a, after(keep_b, pieces[-1]) + got_b]
    both = jnp.stack([s.reshape(units, 8, 2, 64) for s in sums], axis=1)
    weight_grad = both.transpose(0, 1, 3, 2, 4).reshape(units * 32, 64)
    return (jnp.concatenate(pieces, axis=0).reshape(inputs.shape), weight_grad)


def solution(mesh):
    in_specs = (P("gx", "gy", None, None), P("gx", "gy", None, None), P(), P("gx", "gy", None))
    out_specs = (P("gx", "gy", None, None), P("gx", "gy"))
    return jax.shard_map(body, mesh=mesh, in_specs=in_specs, out_specs=out_specs, check_vma=False)
```
